32 devices in a mesh: group: 2 (over x), patch: 16 (over z, y, core).
Axes of the slice: x: 2, y: 2, z: 4, core: 2. Of those that a mesh axis runs over, the one named last changes fastest.
Arguments:
- queries: bfloat16 [40960, 256], P(('group', 'patch')), parts along dimension 0, may hold values from -38 to 38
- key_rows: bfloat16 [40960, 256], P(('group', 'patch')), parts along dimension 0, may hold values from -38 to 38
- value_rows: bfloat16 [40960, 256], P(('group', 'patch')), parts along dimension 0, may hold values from -6 to 6
- grad_out: bfloat16 [40960, 256], P(('group', 'patch')), parts along dimension 0, may hold values from -6 to 6
- window_blocks: int32 [320, 15], P('patch'), may hold values from -1 to 319, as said below
Outputs:
- grad_queries: float32 [40960, 256], P(('group', 'patch')), parts along dimension 0
- grad_keys: float32 [40960, 256], P(('group', 'patch')), parts along dimension 0
- grad_values: float32 [40960, 256], P(('group', 'patch')), parts along dimension 0
The draws below stay inside these ranges and needn't reach their ends.
There are 2 independent parts, one for each index of `group`. The reference program is written for one: setup_inputs(seed, part) draws one part's arguments, and reference() takes and returns one part's arrays. A program takes and returns all parts, laid end to end along the dimension named above; an argument that names none is the same for every part. Nothing has to cross between parts.
Inputs may be any that keep to these rules, and one draw needn't show every extreme that they name: `window_blocks`: row b lists the key blocks of query block b, which lies in stripe b // 20 at block row b % 20. Its live entries are distinct and come first, the rest are -1. Each live entry is a block whose block row differs from the query's by at most one and whose stripe is within two of the query's around the longitude circle, or, for a query in the first or last block row, the block of the same block row in the stripe 16 // 2 away. Some query blocks have all 15 entries live.
All inputs are finite; a program needn't handle non-finite values.
Results may differ from the reference program's by a relative error of at most 0.011.
Values may be sent and summed in bfloat16 or wider, within the bound.
A program may use at most 128 MiB of HBM per device.

```python
import jax
import jax.numpy as jnp
from jax import lax

D = 256
HEADS = 8
HEIGHT = 160
BR = 8
MAXKV = 15
BLK = 64
TOKENS = 20480
NBLK = 320
N_PATCH = 16


def draw_queries(key, part):
    key = jax.random.fold_in(key, 21)
    return jnp.clip(jax.random.normal(key, (TOKENS, D), jnp.float32), -6.0, 6.0).astype(jnp.bfloat16)


def draw_key_rows(key, part):
    key = jax.random.fold_in(key, 22)
    return jnp.clip(jax.random.normal(key, (TOKENS, D), jnp.float32), -6.0, 6.0).astype(jnp.bfloat16)


def draw_window_blocks(key, part):
    key = jax.random.fold_in(key, 3)
    band_count = HEIGHT // BR
    block_index = jnp.arange(NBLK, dtype=jnp.int32)
    stripe = block_index // band_count
    band = block_index % band_count
    pole_dist = jnp.minimum(band, band_count - 1 - band)
    widen = jax.random.randint(jax.random.fold_in(key, 1), (NBLK,), 0, 2)
    widen = jnp.where((stripe == 0) & (band == 1), 1, widen)
    span = jnp.where(pole_dist == 0, 2, 1 + widen)
    slot_index = jnp.arange(16, dtype=jnp.int32)
    row_step = slot_index // 5 - 1
    col_step = slot_index % 5 - 2
    key_band = band[:, None] + row_step[None, :]
    key_stripe = (stripe[:, None] + col_step[None, :]) % N_PATCH
    regular = (slot_index[None, :] < 15) & (key_band >= 0) & (key_band < band_count)
    regular = regular & (jnp.abs(col_step)[None, :] <= span[:, None])
    crossing = (slot_index[None, :] == 15) & (pole_dist == 0)[:, None]
    cross_id = (stripe + N_PATCH // 2) % N_PATCH * band_count + band
    chosen = jnp.where(regular, key_stripe * band_count + key_band, jnp.where(crossing, cross_id[:, None], -1))
    inside = regular | crossing
    jitter = jax.random.randint(jax.random.fold_in(key, 2), (NBLK, 16), 0, 1 << 20)
    order_key = jitter * 16 + slot_index[None, :] + jnp.where(inside, 0, 1 << 26)
    ranked = jnp.argsort(order_key, axis=1, stable=True)
    listed = jnp.take_along_axis(chosen, ranked, axis=1)
    return listed[:, :MAXKV].astype(jnp.int32)


def level_of(own_key, shape, split, smallest, largest):
    level = 1.0
    for dim, shards_of in split:
        draws = jax.random.uniform(jax.random.fold_in(jax.random.fold_in(own_key, 6), dim), (shards_of,), jnp.float32, smallest / len(split), largest / len(split))
        level = level * jnp.repeat(jnp.exp(draws), shape[dim] // shards_of).reshape((-1,) + (1,) * (len(shape) - 1 - dim))
    return level


def bell_draw(rng, shape, spread, bound, split=(), kind=jnp.bfloat16):
    array = jax.random.normal(rng, shape, jnp.float32) * spread
    if len(split) > 0:
        array = level_of(rng, shape, split, -0.22, 0.18) * array
    return jnp.clip(array, min=-bound, max=bound).astype(kind)


def setup_inputs(seed: int = 0, part: int = 0) -> dict:
    keys = jax.random.split(jax.random.key(seed), 6)
    own_keys = jax.random.split(jax.random.fold_in(keys[5], part), 6)
    return {
        "queries": draw_queries(jax.random.fold_in(jax.random.fold_in(keys[5], part), 71), part),
        "key_rows": draw_key_rows(jax.random.fold_in(jax.random.fold_in(keys[5], part), 71), part),
        "value_rows": bell_draw(own_keys[2], (TOKENS, D), 1.0, 6.0, ((0, 16),)),
        "grad_out": bell_draw(own_keys[3], (TOKENS, D), 1.0, 6.0, ((0, 16),)),
        "window_blocks": draw_window_blocks(jax.random.fold_in(keys[5], 71), part),
    }


def attend(query_blk, dout_blk, key_blk, value_blk, live_keys):
    row_count, features = query_blk.shape
    head_size = features // HEADS
    scaling = head_size ** -0.5
    q_heads = query_blk.reshape(row_count, HEADS, head_size).astype(jnp.float32)
    d_heads = dout_blk.reshape(row_count, HEADS, head_size).astype(jnp.float32)
    k_heads = key_blk.reshape(-1, HEADS, head_size).astype(jnp.float32)
    v_heads = value_blk.reshape(-1, HEADS, head_size).astype(jnp.float32)
    scores = jnp.einsum("qhd,khd->hqk", q_heads, k_heads) * scaling
    scores = jnp.where(live_keys[None, None, :], scores, jnp.float32(-1e30))
    row_max = jnp.max(scores, axis=2, keepdims=True)
    exp_scores = jnp.exp(scores - row_max)
    weights = exp_scores / jnp.sum(exp_scores, axis=2, keepdims=True)
    low_weights = lax.optimization_barrier(weights.astype(jnp.bfloat16)).astype(jnp.float32)
    attn_out = jnp.einsum("hqk,khd->qhd", low_weights, v_heads)
    row_dots = jnp.sum(d_heads * attn_out, axis=2)
    grad_weights = jnp.einsum("qhd,khd->hqk", d_heads, v_heads)
    grad_scores = weights * (grad_weights - jnp.transpose(row_dots)[:, :, None])
    low_scores = lax.optimization_barrier(grad_scores.astype(jnp.bfloat16)).astype(jnp.float32)
    grad_q = jnp.einsum("hqk,khd->qhd", low_scores, k_heads) * scaling
    grad_k = jnp.einsum("hqk,qhd->khd", low_scores, q_heads) * scaling
    grad_v = jnp.einsum("hqk,qhd->khd", low_weights, d_heads)
    return grad_q.reshape(row_count, features), grad_k.reshape(-1, features), grad_v.reshape(-1, features)


def reference(queries, key_rows, value_rows, grad_out, window_blocks):
    features = queries.shape[1]
    query_blocks = queries.reshape(NBLK, BLK, features)
    dout_blocks = grad_out.reshape(NBLK, BLK, features)
    key_blocks = key_rows.reshape(NBLK, BLK, features)
    value_blocks = value_rows.reshape(NBLK, BLK, features)

    def advance(totals, packed):
        query_blk, dout_blk, block_ids = packed
        live_keys = jnp.repeat(block_ids >= 0, BLK)
        safe_ids = jnp.where(block_ids >= 0, block_ids, 0).astype(jnp.int32)
        key_blk = key_blocks[safe_ids].reshape(MAXKV * BLK, features)
        value_blk = value_blocks[safe_ids].reshape(MAXKV * BLK, features)
        grad_q, grad_k, grad_v = attend(query_blk, dout_blk, key_blk, value_blk, live_keys)
        totals = totals.at[0, safe_ids].add(grad_k.reshape(MAXKV, BLK, features))
        totals = totals.at[1, safe_ids].add(grad_v.reshape(MAXKV, BLK, features))
        return totals, grad_q

    zero_totals = jnp.zeros((2, NBLK, BLK, features), jnp.float32)
    totals, grad_rows = lax.scan(advance, zero_totals, (query_blocks, dout_blocks, window_blocks))
    grad_queries = grad_rows.reshape(TOKENS, features)
    grad_keys = totals[0].reshape(TOKENS, features)
    grad_values = totals[1].reshape(TOKENS, features)
    return (grad_queries, grad_keys, grad_values)
```

```python
import functools
import math

import jax
import jax.numpy as jnp
from jax import lax
from jax.experimental import pallas as pl
from jax.experimental.pallas import tpu as pltpu
from jax.sharding import PartitionSpec as P

HEADS = 8
REACH = 2
SLOTS = 2 * REACH + 1


def shifted(block, distance):
    n = lax.axis_size("patch")
    return lax.ppermute(block, "patch", [((i - distance) % n, i) for i in range(n)])


def swapped(block):
    n = lax.axis_size("patch")
    return lax.ppermute(block, "patch", [(i, i ^ 1) for i in range(n)])


def block_diagonal(rows):
    head = lax.broadcasted_iota(jnp.int32, rows.shape, 1) // (rows.shape[1] // HEADS)
    zero = jnp.zeros_like(rows)
    return jnp.concatenate([jnp.where(head == h, rows, zero) for h in range(HEADS)], axis=0)


def dot(a, b, dim_a, dim_b):
    return lax.dot_general(
        a, b, (((dim_a,), (dim_b,)), ((), ())), preferred_element_type=jnp.float32
    )


def attend_band(band, block, bias, queries, grad_out, kv, totals, grad_queries, probs, grads):
    features = queries.shape[1]
    scale = (features // HEADS) ** (-0.5)
    rows = pl.ds(pl.multiple_of(band * block, block), block)
    window = pl.ds(pl.multiple_of(band * block, block), 3 * block)
    q = block_diagonal(queries[rows, :])
    d = block_diagonal(grad_out[rows, :])
    top = None
    for slot in range(SLOTS):
        raw = dot(kv[slot, 0, window, :], q, 1, 1) * jnp.float32(scale * math.log2(math.e))
        for part in range(3):
            piece = raw[part * block : (part + 1) * block] + bias[band, slot * 3 + part]
            probs[(slot * 3 + part) * block : (slot * 3 + part + 1) * block, :] = piece
            peak = jnp.max(piece, axis=0, keepdims=True)
            top = peak if top is None else jnp.maximum(top, peak)
    norm = jnp.zeros_like(top)
    row_dot = jnp.zeros_like(top)
    for slot in range(SLOTS):
        span = slice(slot * 3 * block, (slot + 1) * 3 * block)
        p = jnp.exp2(probs[span, :] - top)
        g = dot(kv[slot, 1, window, :], d, 1, 1)
        norm += jnp.sum(p, axis=0, keepdims=True)
        row_dot += jnp.sum(p * g, axis=0, keepdims=True)
        probs[span, :] = p
        grads[span, :] = g
    inverse = 1.0 / norm
    row_dot = row_dot * inverse
    grad_q = None
    for slot in range(SLOTS):
        span = slice(slot * 3 * block, (slot + 1) * 3 * block)
        w = probs[span, :] * inverse
        g = (w * (grads[span, :] - row_dot)).astype(jnp.bfloat16)
        totals[slot, 1, window, :] += dot(w.astype(jnp.bfloat16), d, 1, 0)
        totals[slot, 0, window, :] += dot(g, q, 1, 0)
        term = dot(kv[slot, 0, window, :], g, 0, 0)
        grad_q = term if grad_q is None else grad_q + term
    head_row = lax.broadcasted_iota(jnp.int32, grad_q.shape, 0) // (features // HEADS)
    head_col = lax.broadcasted_iota(jnp.int32, grad_q.shape, 1) // block
    grad_q = jnp.where(head_row == head_col, grad_q, 0.0)
    pair = 2 * block
    folded = grad_q[:, :pair]
    for at in range(pair, HEADS * block, pair):
        folded = folded + grad_q[:, at : at + pair]
    folded = folded.T
    grad_queries[rows, :] = (folded[:block] + folded[block:]) * scale


def kernel(block, bias, queries, grad_out, kv, grad_queries, totals, probs, grads):
    totals[...] = jnp.zeros_like(totals)

    def step(band, carry):
        attend_band(band, block, bias, queries, grad_out, kv, totals, grad_queries, probs, grads)
        return carry

    lax.fori_loop(0, queries.shape[0] // block, step, 0)


def bias_of(window_blocks):
    bands = window_blocks.shape[0]
    stripes = lax.axis_size("patch")
    stripe = lax.axis_index("patch")
    band = jnp.arange(bands, dtype=jnp.int32)[:, None, None]
    slot = jnp.arange(SLOTS, dtype=jnp.int32)[None, :, None]
    row = band + jnp.arange(-1, 2, dtype=jnp.int32)[None, None, :]
    inside = (row >= 0) & (row < bands)
    regular = (stripe + slot - REACH) % stripes * bands + row
    across = jnp.where(slot == REACH, (stripe + stripes // 2) % stripes * bands + band, -2)
    wanted = jnp.where(inside, regular, across)
    live = jnp.any(wanted[..., None] == window_blocks[:, None, None, :], axis=-1)
    return jnp.where(live, 0.0, -1e30).astype(jnp.float32).reshape(bands, SLOTS * 3)


def local(queries, key_rows, value_rows, grad_out, window_blocks):
    tokens, features = queries.shape
    bands = window_blocks.shape[0]
    block = tokens // bands
    half_turn = lax.axis_size("patch") // 2
    even = lax.axis_index("patch") % 2 == 0
    bias = bias_of(window_blocks)
    own = jnp.stack([key_rows, value_rows])
    after = shifted(own, -2)
    before = shifted(own, 2)
    near = swapped(own)
    far = swapped(jnp.where(even, after, before))
    poles = shifted(jnp.concatenate([own[:, :block], own[:, tokens - block :]], axis=1), half_turn)
    pad = lambda x: jnp.pad(x, ((0, 0), (block, block), (0, 0)))
    kv = jnp.stack(
        [
            pad(before),
            pad(jnp.where(even, far, near)),
            jnp.concatenate([poles[:, :block], own, poles[:, block:]], axis=1),
            pad(jnp.where(even, near, far)),
            pad(after),
        ]
    )
    vmem = pl.BlockSpec(memory_space=pltpu.VMEM)
    grad_rows, totals = pl.pallas_call(
        functools.partial(kernel, block),
        out_shape=(
            jax.ShapeDtypeStruct((tokens, features), jnp.float32),
            jax.ShapeDtypeStruct(kv.shape, jnp.float32),
        ),
        in_specs=[pl.BlockSpec(memory_space=pltpu.SMEM), vmem, vmem, vmem],
        out_specs=(vmem, vmem),
        scratch_shapes=[
            pltpu.VMEM((SLOTS * 3 * block, HEADS * block), jnp.float32),
            pltpu.VMEM((SLOTS * 3 * block, HEADS * block), jnp.float32),
        ],
        compiler_params=pltpu.CompilerParams(vmem_limit_bytes=56 * 2**20),
    )(bias, queries, grad_out, kv)
    scale = jnp.array([(features // HEADS) ** (-0.5), 1.0], jnp.float32)[:, None, None]
    totals = totals * scale
    inner = totals[:, :, block : block + tokens]
    low = inner.astype(jnp.bfloat16)
    far = swapped(jnp.where(even, low[1], low[3])).astype(jnp.float32)
    zero = jnp.zeros_like(far)
    to_after = (inner[4] + jnp.where(even, far, zero)).astype(jnp.bfloat16)
    to_before = (inner[0] + jnp.where(even, zero, far)).astype(jnp.bfloat16)
    near = swapped(jnp.where(even, low[3], low[1])).astype(jnp.float32)
    pole_parts = jnp.concatenate([totals[2, :, :block], totals[2, :, block + tokens :]], axis=1)
    pole_back = shifted(pole_parts.astype(jnp.bfloat16), half_turn).astype(jnp.float32)
    owned = (
        inner[2]
        + near
        + shifted(to_after, 2).astype(jnp.float32)
        + shifted(to_before, -2).astype(jnp.float32)
    )
    owned = owned.at[:, :block].add(pole_back[:, :block])
    owned = owned.at[:, tokens - block :].add(pole_back[:, block:])
    return grad_rows, owned[0], owned[1]


def solution(mesh):
    spec = P(("group", "patch"), None)
    return jax.shard_map(
        local,
        mesh=mesh,
        in_specs=(spec, spec, spec, spec, P("patch", None)),
        out_specs=(spec, spec, spec),
        check_vma=False,
    )
```

```python
import functools
import math

import jax
import jax.numpy as jnp
from jax import lax
from jax.experimental import pallas as pl
from jax.experimental.pallas import tpu as pltpu
from jax.sharding import PartitionSpec as P

HEADS = 8
REACH = 2
SLOTS = 2 * REACH + 1


def block_diagonal(rows):
    head = lax.broadcasted_iota(jnp.int32, rows.shape, 1) // (rows.shape[1] // HEADS)
    zero = jnp.zeros_like(rows)
    return jnp.concatenate([jnp.where(head == h, rows, zero) for h in range(HEADS)], axis=0)


def dot(a, b, dim_a, dim_b):
    return lax.dot_general(
        a, b, (((dim_a,), (dim_b,)), ((), ())), preferred_element_type=jnp.float32
    )


def attend_band(band, block, bias, queries, grad_out, kv, totals, grad_queries, probs, grads):
    features = queries.shape[1]
    scale = (features // HEADS) ** (-0.5)
    rows = pl.ds(pl.multiple_of(band * block, block), block)
    window = pl.ds(pl.multiple_of(band * block, block), 3 * block)
    q = block_diagonal(queries[rows, :])
    d = block_diagonal(grad_out[rows, :])
    top = None
    for slot in range(SLOTS):
        raw = dot(kv[slot, 0, window, :], q, 1, 1) * jnp.float32(scale * math.log2(math.e))
        for part in range(3):
            piece = raw[part * block : (part + 1) * block] + bias[band, slot * 3 + part]
            probs[(slot * 3 + part) * block : (slot * 3 + part + 1) * block, :] = piece
            peak = jnp.max(piece, axis=0, keepdims=True)
            top = peak if top is None else jnp.maximum(top, peak)
    norm = jnp.zeros_like(top)
    row_dot = jnp.zeros_like(top)
    for slot in range(SLOTS):
        span = slice(slot * 3 * block, (slot + 1) * 3 * block)
        p = jnp.exp2(probs[span, :] - top)
        g = dot(kv[slot, 1, window, :], d, 1, 1)
        norm += jnp.sum(p, axis=0, keepdims=True)
        row_dot += jnp.sum(p * g, axis=0, keepdims=True)
        probs[span, :] = p
        grads[span, :] = g
    inverse = 1.0 / norm
    row_dot = row_dot * inverse
    grad_q = None
    for slot in range(SLOTS):
        span = slice(slot * 3 * block, (slot + 1) * 3 * block)
        w = probs[span, :] * inverse
        g = (w * (grads[span, :] - row_dot)).astype(jnp.bfloat16)
        totals[slot, 1, window, :] += dot(w.astype(jnp.bfloat16), d, 1, 0)
        totals[slot, 0, window, :] += dot(g, q, 1, 0)
        term = dot(kv[slot, 0, window, :], g, 0, 0)
        grad_q = term if grad_q is None else grad_q + term
    head_row = lax.broadcasted_iota(jnp.int32, grad_q.shape, 0) // (features // HEADS)
    head_col = lax.broadcasted_iota(jnp.int32, grad_q.shape, 1) // block
    grad_q = jnp.where(head_row == head_col, grad_q, 0.0)
    pair = 2 * block
    folded = grad_q[:, :pair]
    for at in range(pair, HEADS * block, pair):
        folded = folded + grad_q[:, at : at + pair]
    folded = folded.T
    grad_queries[rows, :] = (folded[:block] + folded[block:]) * scale


def kernel(
    block,
    bias,
    queries,
    grad_out,
    key_rows,
    value_rows,
    grad_queries,
    grad_keys,
    grad_values,
    kv,
    totals,
    probs,
    grads,
    far_out,
    far_in,
    near_out,
    near_in,
    merged_out,
    merged_in,
    plain_out,
    plain_in,
    pole_out,
    pole_in,
    send,
    recv,
    pole_send,
    pole_recv,
):
    tokens, features = queries.shape
    bands = tokens // block
    scale = (features // HEADS) ** (-0.5)
    n = lax.axis_size("patch")
    me = lax.axis_index("patch")
    odd = lax.rem(me, 2)
    partner = me + 1 - 2 * odd
    after = lax.rem(me + REACH, n)
    before = lax.rem(me + n - REACH, n)
    across = lax.rem(me + n // 2, n)
    last = 2 * REACH

    def at(band):
        return pl.ds(pl.multiple_of(band * block, block), block)

    def padded(band):
        return at(band + 1)

    def remote(source, target, stream, band, device):
        return pltpu.make_async_remote_copy(
            src_ref=source,
            dst_ref=target,
            send_sem=send.at[stream, band],
            recv_sem=recv.at[stream, band],
            device_id={"patch": device},
            device_id_type=pl.DeviceIdType.MESH,
        )

    def keys_after(band):
        own = kv.at[REACH, :, padded(band), :]
        return remote(own, kv.at[0, :, padded(band), :], 0, band, after)

    def keys_before(band):
        own = kv.at[REACH, :, padded(band), :]
        return remote(own, kv.at[last, :, padded(band), :], 1, band, before)

    def keys_near(band):
        own = kv.at[REACH, :, padded(band), :]
        return remote(own, kv.at[1 + 2 * odd, :, padded(band), :], 2, band, partner)

    def keys_far(band):
        fetched = kv.at[last - last * odd, :, padded(band), :]
        return remote(fetched, kv.at[3 - 2 * odd, :, padded(band), :], 3, band, partner)

    def sums_far(band):
        return remote(far_out.at[:, at(band), :], far_in.at[:, at(band), :], 4, band, partner)

    def sums_near(band):
        return remote(near_out.at[:, at(band), :], near_in.at[:, at(band), :], 5, band, partner)

    def sums_merged(band):
        device = lax.rem(me + n + REACH - 2 * REACH * odd, n)
        return remote(merged_out.at[:, at(band), :], merged_in.at[:, at(band), :], 6, band, device)

    def sums_plain(band):
        device = lax.rem(me + n - REACH + 2 * REACH * odd, n)
        return remote(plain_out.at[:, at(band), :], plain_in.at[:, at(band), :], 7, band, device)

    def pole_copy(source, target, which):
        return pltpu.make_async_remote_copy(
            src_ref=source,
            dst_ref=target,
            send_sem=pole_send.at[which],
            recv_sem=pole_recv.at[which],
            device_id={"patch": across},
            device_id_type=pl.DeviceIdType.MESH,
        )

    def pole_keys(which):
        edge = 0 if which == 0 else bands - 1
        beyond = -1 if which == 0 else bands
        return pole_copy(kv.at[REACH, :, padded(edge), :], kv.at[REACH, :, padded(beyond), :], which)

    def pole_sums(which):
        return pole_copy(pole_out.at[which], pole_in.at[which], 2 + which)

    def each_band(body):
        def step(band, carry):
            body(band)
            return carry

        lax.fori_loop(0, bands, step, 0)

    def scaled(part, value):
        return value * jnp.float32(scale) if part == 0 else value

    barrier = pltpu.get_barrier_semaphore()
    for device in (after, before, partner, across):
        pl.semaphore_signal(
            barrier, inc=1, device_id={"patch": device}, device_id_type=pl.DeviceIdType.MESH
        )
    kv[REACH, 0, block : block + tokens, :] = key_rows[...]
    kv[REACH, 1, block : block + tokens, :] = value_rows[...]
    pl.semaphore_wait(barrier, 4)

    pole_keys(0).start()

    @each_band
    def _(band):
        keys_after(band).start()
        keys_before(band).start()
        keys_near(band).start()

    pole_keys(1).start()

    blank = jnp.zeros((2, block, features), kv.dtype)
    for slot in range(SLOTS):
        if slot != REACH:
            kv[slot, :, :block, :] = blank
            kv[slot, :, block + tokens :, :] = blank
    for slot in range(SLOTS):
        for part in range(2):
            totals[slot, part] = jnp.zeros(totals.shape[2:], jnp.float32)

    def step(t, carry):
        @pl.when(t < bands)
        def _():
            keys_after(t).wait_recv()
            keys_before(t).wait_recv()
            keys_far(t).start()

        @pl.when((t >= 1) & (t <= bands))
        def _():
            keys_near(t - 1).wait_recv()
            keys_far(t - 1).wait_recv()

        @pl.when(t == 2)
        def _():
            pole_keys(0).wait_recv()

        @pl.when(t == bands + 1)
        def _():
            pole_keys(1).wait_recv()

        @pl.when((t >= 2) & (t <= bands + 1))
        def _():
            attend_band(
                t - 2, block, bias, queries, grad_out, kv, totals, grad_queries, probs, grads
            )

        @pl.when((t >= 3) & (t <= bands + 2))
        def _():
            band = t - 3
            for part in range(2):
                far = scaled(part, totals[1 + 2 * odd, part, padded(band), :])
                far_out[part, at(band), :] = far.astype(jnp.bfloat16)
                near = scaled(part, totals[3 - 2 * odd, part, padded(band), :])
                near_out[part, at(band), :] = near.astype(jnp.bfloat16)
            sums_far(band).start()
            sums_near(band).start()

        @pl.when(t >= 4)
        def _():
            band = t - 4
            sums_far(band).wait_recv()
            for part in range(2):
                merged = scaled(part, totals[last - last * odd, part, padded(band), :])
                merged = merged + far_in[part, at(band), :].astype(jnp.float32)
                merged_out[part, at(band), :] = merged.astype(jnp.bfloat16)
                plain = scaled(part, totals[last * odd, part, padded(band), :])
                plain_out[part, at(band), :] = plain.astype(jnp.bfloat16)
            sums_merged(band).start()
            sums_plain(band).start()

        return carry

    lax.fori_loop(0, bands + 4, step, 0)

    for which, beyond in ((0, -1), (1, bands)):
        for part in range(2):
            value = scaled(part, totals[REACH, part, padded(beyond), :])
            pole_out[which, part] = value.astype(jnp.bfloat16)
        pole_sums(which).start()

    @each_band
    def _(band):
        sums_near(band).wait_recv()
        sums_merged(band).wait_recv()
        sums_plain(band).wait_recv()
        for part, result in ((0, grad_keys), (1, grad_values)):
            value = scaled(part, totals[REACH, part, padded(band), :])
            for arrived in (near_in, merged_in, plain_in):
                value = value + arrived[part, at(band), :].astype(jnp.float32)
            result[at(band), :] = value

    for which, edge in ((0, 0), (1, bands - 1)):
        pole_sums(which).wait_recv()
        for part, result in ((0, grad_keys), (1, grad_values)):
            result[at(edge), :] += pole_in[which, part].astype(jnp.float32)

    @each_band
    def _(band):
        for copy in (keys_after, keys_before, keys_near, keys_far):
            copy(band).wait_send()
        for copy in (sums_far, sums_near, sums_merged, sums_plain):
            copy(band).wait_send()

    for which in range(2):
        pole_keys(which).wait_send()
        pole_sums(which).wait_send()


def bias_of(window_blocks):
    bands = window_blocks.shape[0]
    stripes = lax.axis_size("patch")
    stripe = lax.axis_index("patch")
    band = jnp.arange(bands, dtype=jnp.int32)[:, None, None]
    slot = jnp.arange(SLOTS, dtype=jnp.int32)[None, :, None]
    row = band + jnp.arange(-1, 2, dtype=jnp.int32)[None, None, :]
    inside = (row >= 0) & (row < bands)
    regular = (stripe + slot - REACH) % stripes * bands + row
    across = jnp.where(slot == REACH, (stripe + stripes // 2) % stripes * bands + band, -2)
    wanted = jnp.where(inside, regular, across)
    live = jnp.any(wanted[..., None] == window_blocks[:, None, None, :], axis=-1)
    return jnp.where(live, 0.0, -1e30).astype(jnp.float32).reshape(bands, SLOTS * 3)


def local(queries, key_rows, value_rows, grad_out, window_blocks):
    tokens, features = queries.shape
    bands = window_blocks.shape[0]
    block = tokens // bands
    vmem = pl.BlockSpec(memory_space=pltpu.VMEM)
    result = jax.ShapeDtypeStruct((tokens, features), jnp.float32)
    padded = tokens + 2 * block
    wide = pltpu.VMEM((SLOTS * 3 * block, HEADS * block), jnp.float32)
    travelling = pltpu.VMEM((2, tokens, features), jnp.bfloat16)
    pole = pltpu.VMEM((2, 2, block, features), jnp.bfloat16)
    return pl.pallas_call(
        functools.partial(kernel, block),
        out_shape=(result, result, result),
        in_specs=[pl.BlockSpec(memory_space=pltpu.SMEM), vmem, vmem, vmem, vmem],
        out_specs=(vmem, vmem, vmem),
        scratch_shapes=[
            pltpu.VMEM((SLOTS, 2, padded, features), jnp.bfloat16),
            pltpu.VMEM((SLOTS, 2, padded, features), jnp.float32),
            wide,
            wide,
            *([travelling] * 8),
            pole,
            pole,
            pltpu.SemaphoreType.DMA((8, bands)),
            pltpu.SemaphoreType.DMA((8, bands)),
            pltpu.SemaphoreType.DMA((4,)),
            pltpu.SemaphoreType.DMA((4,)),
        ],
        compiler_params=pltpu.CompilerParams(
            collective_id=0, has_side_effects=True, vmem_limit_bytes=60 * 2**20
        ),
    )(bias_of(window_blocks), queries, grad_out, key_rows, value_rows)


def solution(mesh):
    spec = P(("group", "patch"), None)
    return jax.shard_map(
        local,
        mesh=mesh,
        in_specs=(spec, spec, spec, spec, P("patch", None)),
        out_specs=(spec, spec, spec),
        check_vma=False,
    )
```

```python
import functools
import math

import jax
import jax.numpy as jnp
from jax import lax
from jax.experimental import pallas as pl
from jax.experimental.pallas import tpu as pltpu
from jax.sharding import PartitionSpec as P

HEADS = 8
REACH = 2
SLOTS = 2 * REACH + 1


def block_diagonal(rows):
    head = lax.broadcasted_iota(jnp.int32, rows.shape, 1) // (rows.shape[1] // HEADS)
    zero = jnp.zeros_like(rows)
    return jnp.concatenate([jnp.where(head == h, rows, zero) for h in range(HEADS)], axis=0)


def dot(a, b, dim_a, dim_b):
    return lax.dot_general(
        a, b, (((dim_a,), (dim_b,)), ((), ())), preferred_element_type=jnp.float32
    )


def attend_band(band, block, bias, queries, grad_out, kv, totals, grad_queries, probs, grads):
    features = queries.shape[1]
    scale = (features // HEADS) ** (-0.5)
    rows = pl.ds(pl.multiple_of(band * block, block), block)
    window = pl.ds(pl.multiple_of(band * block, block), 3 * block)
    q = block_diagonal(queries[rows, :])
    d = block_diagonal(grad_out[rows, :])
    top = None
    for slot in range(SLOTS):
        raw = dot(kv[slot, 0, window, :], q, 1, 1) * jnp.float32(scale * math.log2(math.e))
        for part in range(3):
            piece = raw[part * block : (part + 1) * block] + bias[band, slot * 3 + part]
            probs[(slot * 3 + part) * block : (slot * 3 + part + 1) * block, :] = piece
            peak = jnp.max(piece, axis=0, keepdims=True)
            top = peak if top is None else jnp.maximum(top, peak)
    norm = jnp.zeros_like(top)
    row_dot = jnp.zeros_like(top)
    for slot in range(SLOTS):
        span = slice(slot * 3 * block, (slot + 1) * 3 * block)
        p = jnp.exp2(probs[span, :] - top)
        g = dot(kv[slot, 1, window, :], d, 1, 1)
        norm += jnp.sum(p, axis=0, keepdims=True)
        row_dot += jnp.sum(p * g, axis=0, keepdims=True)
        probs[span, :] = p
        grads[span, :] = g
    inverse = 1.0 / norm
    row_dot = row_dot * inverse
    grad_q = None
    for slot in range(SLOTS):
        span = slice(slot * 3 * block, (slot + 1) * 3 * block)
        w = probs[span, :] * inverse
        g = (w * (grads[span, :] - row_dot)).astype(jnp.bfloat16)
        totals[slot, 1, window, :] += dot(w.astype(jnp.bfloat16), d, 1, 0)
        totals[slot, 0, window, :] += dot(g, q, 1, 0)
        term = dot(kv[slot, 0, window, :], g, 0, 0)
        grad_q = term if grad_q is None else grad_q + term
    head_row = lax.broadcasted_iota(jnp.int32, grad_q.shape, 0) // (features // HEADS)
    head_col = lax.broadcasted_iota(jnp.int32, grad_q.shape, 1) // block
    grad_q = jnp.where(head_row == head_col, grad_q, 0.0)
    pair = 2 * block
    folded = grad_q[:, :pair]
    for at in range(pair, HEADS * block, pair):
        folded = folded + grad_q[:, at : at + pair]
    folded = folded.T
    grad_queries[rows, :] = (folded[:block] + folded[block:]) * scale


def kernel(
    block,
    bias,
    queries,
    grad_out,
    key_rows,
    value_rows,
    grad_queries,
    grad_keys,
    grad_values,
    kv,
    totals,
    probs,
    grads,
    far_in,
    near_in,
    relay_out,
    relay_in,
    mate_out,
    mate_in,
    pole_out,
    pole_in,
    send,
    recv,
    pole_send,
    pole_recv,
):
    tokens, features = queries.shape
    bands = tokens // block
    scale = (features // HEADS) ** (-0.5)
    n = lax.axis_size("patch")
    me = lax.axis_index("patch")
    odd = lax.rem(me, 2)
    side = lax.rem(me // 2, 2)
    partner = me + 1 - 2 * odd
    mate = me + 2 - 4 * side
    ahead = lax.rem(me + 4, n)
    behind = lax.rem(me + n - 4, n)
    across = lax.rem(me + n // 2, n)
    last = 2 * REACH
    mate_slot = last - last * side
    relay_slot = last * side

    def at(band):
        return pl.ds(pl.multiple_of(band * block, block), block)

    def padded(band):
        return at(band + 1)

    def remote(source, target, stream, band, device):
        return pltpu.make_async_remote_copy(
            src_ref=source,
            dst_ref=target,
            send_sem=send.at[stream, band],
            recv_sem=recv.at[stream, band],
            device_id={"patch": device},
            device_id_type=pl.DeviceIdType.MESH,
        )

    def keys_mate(band):
        own = kv.at[REACH, :, padded(band), :]
        return remote(own, kv.at[relay_slot, :, padded(band), :], 0, band, mate)

    def keys_relay(band):
        device = lax.rem(me + n + 4 - 8 * side, n)
        fetched = kv.at[mate_slot, :, padded(band), :]
        return remote(fetched, kv.at[relay_slot, :, padded(band), :], 1, band, device)

    def keys_near(band):
        own = kv.at[REACH, :, padded(band), :]
        return remote(own, kv.at[1 + 2 * odd, :, padded(band), :], 2, band, partner)

    def keys_far(band):
        fetched = kv.at[last - last * odd, :, padded(band), :]
        return remote(fetched, kv.at[3 - 2 * odd, :, padded(band), :], 3, band, partner)

    def sums_far(band):
        source = totals.at[1 + 2 * odd, :, padded(band), :]
        return remote(source, far_in.at[:, at(band), :], 4, band, partner)

    def sums_near(band):
        source = totals.at[3 - 2 * odd, :, padded(band), :]
        return remote(source, near_in.at[:, at(band), :], 5, band, partner)

    def sums_relay(band):
        device = lax.rem(me + n - 4 + 8 * side, n)
        return remote(relay_out.at[:, at(band), :], relay_in.at[:, at(band), :], 6, band, device)

    def sums_mate(band):
        return remote(mate_out.at[:, at(band), :], mate_in.at[:, at(band), :], 7, band, mate)

    def pole_copy(source, target, which):
        return pltpu.make_async_remote_copy(
            src_ref=source,
            dst_ref=target,
            send_sem=pole_send.at[which],
            recv_sem=pole_recv.at[which],
            device_id={"patch": across},
            device_id_type=pl.DeviceIdType.MESH,
        )

    def pole_keys(which):
        edge = 0 if which == 0 else bands - 1
        beyond = -1 if which == 0 else bands
        return pole_copy(kv.at[REACH, :, padded(edge), :], kv.at[REACH, :, padded(beyond), :], which)

    def pole_sums(which):
        return pole_copy(pole_out.at[which], pole_in.at[which], 2 + which)

    def each_band(body):
        def step(band, carry):
            body(band)
            return carry

        lax.fori_loop(0, bands, step, 0)

    def scaled(part, value):
        return value * jnp.float32(scale) if part == 0 else value

    barrier = pltpu.get_barrier_semaphore()
    for device in (mate, partner, ahead, behind, across):
        pl.semaphore_signal(
            barrier, inc=1, device_id={"patch": device}, device_id_type=pl.DeviceIdType.MESH
        )
    kv[REACH, 0, block : block + tokens, :] = key_rows[...]
    kv[REACH, 1, block : block + tokens, :] = value_rows[...]
    pl.semaphore_wait(barrier, 5)

    pole_keys(0).start()

    @each_band
    def _(band):
        keys_mate(band).start()
        keys_near(band).start()

    pole_keys(1).start()

    blank = jnp.zeros((2, block, features), kv.dtype)
    for slot in range(SLOTS):
        if slot != REACH:
            kv[slot, :, :block, :] = blank
            kv[slot, :, block + tokens :, :] = blank
    for slot in range(SLOTS):
        for part in range(2):
            totals[slot, part] = jnp.zeros(totals.shape[2:], jnp.float32)

    def send_pole_sums(which, beyond):
        for part in range(2):
            value = scaled(part, totals[REACH, part, padded(beyond), :])
            pole_out[which, part] = value.astype(jnp.bfloat16)
        pole_sums(which).start()

    def step(t, carry):
        @pl.when(t < bands)
        def _():
            keys_mate(t).wait_recv()
            keys_relay(t).start()

        @pl.when((t >= 1) & (t <= bands))
        def _():
            keys_near(t - 1).wait_recv()
            keys_relay(t - 1).wait_recv()
            keys_far(t - 1).start()

        @pl.when((t >= 2) & (t <= bands + 1))
        def _():
            keys_far(t - 2).wait_recv()

        @pl.when(t == 3)
        def _():
            pole_keys(0).wait_recv()

        @pl.when(t == bands + 2)
        def _():
            pole_keys(1).wait_recv()

        @pl.when((t >= 3) & (t <= bands + 2))
        def _():
            attend_band(
                t - 3, block, bias, queries, grad_out, kv, totals, grad_queries, probs, grads
            )

        @pl.when(t == 4)
        def _():
            send_pole_sums(0, -1)

        @pl.when(t == bands + 3)
        def _():
            send_pole_sums(1, bands)

        @pl.when((t >= 4) & (t <= bands + 3))
        def _():
            sums_far(t - 4).start()
            sums_near(t - 4).start()

        @pl.when((t >= 5) & (t <= bands + 4))
        def _():
            band = t - 5
            sums_far(band).wait_recv()
            for part in range(2):
                totals[last - last * odd, part, padded(band), :] += far_in[part, at(band), :]
                value = scaled(part, totals[relay_slot, part, padded(band), :])
                relay_out[part, at(band), :] = value.astype(jnp.bfloat16)
            sums_relay(band).start()

        @pl.when(t >= 6)
        def _():
            band = t - 6
            sums_relay(band).wait_recv()
            for part in range(2):
                value = scaled(part, totals[mate_slot, part, padded(band), :])
                value = value + relay_in[part, at(band), :].astype(jnp.float32)
                mate_out[part, at(band), :] = value.astype(jnp.bfloat16)
            sums_mate(band).start()

        return carry

    lax.fori_loop(0, bands + 6, step, 0)

    @each_band
    def _(band):
        sums_near(band).wait_recv()
        sums_mate(band).wait_recv()
        for part, result in ((0, grad_keys), (1, grad_values)):
            value = totals[REACH, part, padded(band), :] + near_in[part, at(band), :]
            arrived = mate_in[part, at(band), :].astype(jnp.float32)
            result[at(band), :] = scaled(part, value) + arrived

    for which, edge in ((0, 0), (1, bands - 1)):
        pole_sums(which).wait_recv()
        for part, result in ((0, grad_keys), (1, grad_values)):
            result[at(edge), :] += pole_in[which, part].astype(jnp.float32)

    @each_band
    def _(band):
        for copy in (keys_mate, keys_relay, keys_near, keys_far):
            copy(band).wait_send()
        for copy in (sums_far, sums_near, sums_relay, sums_mate):
            copy(band).wait_send()

    for which in range(2):
        pole_keys(which).wait_send()
        pole_sums(which).wait_send()


def bias_of(window_blocks):
    bands = window_blocks.shape[0]
    stripes = lax.axis_size("patch")
    stripe = lax.axis_index("patch")
    band = jnp.arange(bands, dtype=jnp.int32)[:, None, None]
    slot = jnp.arange(SLOTS, dtype=jnp.int32)[None, :, None]
    row = band + jnp.arange(-1, 2, dtype=jnp.int32)[None, None, :]
    inside = (row >= 0) & (row < bands)
    regular = (stripe + slot - REACH) % stripes * bands + row
    across = jnp.where(slot == REACH, (stripe + stripes // 2) % stripes * bands + band, -2)
    wanted = jnp.where(inside, regular, across)
    live = jnp.any(wanted[..., None] == window_blocks[:, None, None, :], axis=-1)
    return jnp.where(live, 0.0, -1e30).astype(jnp.float32).reshape(bands, SLOTS * 3)


def local(queries, key_rows, value_rows, grad_out, window_blocks):
    tokens, features = queries.shape
    bands = window_blocks.shape[0]
    block = tokens // bands
    vmem = pl.BlockSpec(memory_space=pltpu.VMEM)
    result = jax.ShapeDtypeStruct((tokens, features), jnp.float32)
    padded = tokens + 2 * block
    wide = pltpu.VMEM((SLOTS * 3 * block, HEADS * block), jnp.float32)
    whole = pltpu.VMEM((2, tokens, features), jnp.float32)
    travelling = pltpu.VMEM((2, tokens, features), jnp.bfloat16)
    pole = pltpu.VMEM((2, 2, block, features), jnp.bfloat16)
    return pl.pallas_call(
        functools.partial(kernel, block),
        out_shape=(result, result, result),
        in_specs=[pl.BlockSpec(memory_space=pltpu.SMEM), vmem, vmem, vmem, vmem],
        out_specs=(vmem, vmem, vmem),
        scratch_shapes=[
            pltpu.VMEM((SLOTS, 2, padded, features), jnp.bfloat16),
            pltpu.VMEM((SLOTS, 2, padded, features), jnp.float32),
            wide,
            wide,
            whole,
            whole,
            *([travelling] * 4),
            pole,
            pole,
            pltpu.SemaphoreType.DMA((8, bands)),
            pltpu.SemaphoreType.DMA((8, bands)),
            pltpu.SemaphoreType.DMA((4,)),
            pltpu.SemaphoreType.DMA((4,)),
        ],
        compiler_params=pltpu.CompilerParams(
            collective_id=0, has_side_effects=True, vmem_limit_bytes=60 * 2**20
        ),
    )(bias_of(window_blocks), queries, grad_out, key_rows, value_rows)


def solution(mesh):
    spec = P(("group", "patch"), None)
    return jax.shard_map(
        local,
        mesh=mesh,
        in_specs=(spec, spec, spec, spec, P("patch", None)),
        out_specs=(spec, spec, spec),
        check_vma=False,
    )
```

```python
import functools
import math

import jax
import jax.numpy as jnp
from jax import lax
from jax.experimental import pallas as pl
from jax.experimental.pallas import tpu as pltpu
from jax.sharding import PartitionSpec as P

HEADS = 8
REACH = 2
SLOTS = 2 * REACH + 1


def block_diagonal(rows):
    head = lax.broadcasted_iota(jnp.int32, rows.shape, 1) // (rows.shape[1] // HEADS)
    zero = jnp.zeros_like(rows)
    return jnp.concatenate([jnp.where(head == h, rows, zero) for h in range(HEADS)], axis=0)


def dot(a, b, dim_a, dim_b):
    return lax.dot_general(
        a, b, (((dim_a,), (dim_b,)), ((), ())), preferred_element_type=jnp.float32
    )


def attend_band(band, block, bias, queries, grad_out, kv, totals, grad_queries, probs, grads):
    features = queries.shape[1]
    scale = (features // HEADS) ** (-0.5)
    rows = pl.ds(pl.multiple_of(band * block, block), block)
    window = pl.ds(pl.multiple_of(band * block, block), 3 * block)
    q = block_diagonal(queries[rows, :])
    d = block_diagonal(grad_out[rows, :])
    top = None
    for slot in range(SLOTS):
        raw = dot(kv[slot, 0, window, :], q, 1, 1) * jnp.float32(scale * math.log2(math.e))
        for part in range(3):
            piece = raw[part * block : (part + 1) * block] + bias[band, slot * 3 + part]
            probs[(slot * 3 + part) * block : (slot * 3 + part + 1) * block, :] = piece
            peak = jnp.max(piece, axis=0, keepdims=True)
            top = peak if top is None else jnp.maximum(top, peak)
    norm = jnp.zeros_like(top)
    row_dot = jnp.zeros_like(top)
    for slot in range(SLOTS):
        span = slice(slot * 3 * block, (slot + 1) * 3 * block)
        p = jnp.exp2(probs[span, :] - top)
        g = dot(kv[slot, 1, window, :], d, 1, 1)
        norm += jnp.sum(p, axis=0, keepdims=True)
        row_dot += jnp.sum(p * g, axis=0, keepdims=True)
        probs[span, :] = p
        grads[span, :] = g
    inverse = 1.0 / norm
    row_dot = row_dot * inverse
    grad_q = None
    for slot in range(SLOTS):
        span = slice(slot * 3 * block, (slot + 1) * 3 * block)
        w = probs[span, :] * inverse
        g = (w * (grads[span, :] - row_dot)).astype(jnp.bfloat16)
        totals[slot, 1, window, :] += dot(w.astype(jnp.bfloat16), d, 1, 0)
        totals[slot, 0, window, :] += dot(g, q, 1, 0)
        term = dot(kv[slot, 0, window, :], g, 0, 0)
        grad_q = term if grad_q is None else grad_q + term
    head_row = lax.broadcasted_iota(jnp.int32, grad_q.shape, 0) // (features // HEADS)
    head_col = lax.broadcasted_iota(jnp.int32, grad_q.shape, 1) // block
    grad_q = jnp.where(head_row == head_col, grad_q, 0.0)
    pair = 2 * block
    folded = grad_q[:, :pair]
    for at in range(pair, HEADS * block, pair):
        folded = folded + grad_q[:, at : at + pair]
    folded = folded.T
    grad_queries[rows, :] = (folded[:block] + folded[block:]) * scale


def kernel(
    block,
    bias,
    queries,
    grad_out,
    key_rows,
    value_rows,
    grad_queries,
    grad_keys,
    grad_values,
    kv,
    totals,
    probs,
    grads,
    far_in,
    near_in,
    relay_out,
    relay_in,
    mate_out,
    mate_in,
    pole_out,
    pole_in,
    send,
    recv,
    pole_send,
    pole_recv,
):
    tokens, features = queries.shape
    bands = tokens // block
    scale = (features // HEADS) ** (-0.5)
    n = lax.axis_size("patch")
    me = lax.axis_index("patch")
    odd = lax.rem(me, 2)
    side = lax.rem(me // 2, 2)
    partner = me + 1 - 2 * odd
    mate = me + 2 - 4 * side
    ahead = lax.rem(me + 4, n)
    behind = lax.rem(me + n - 4, n)
    across = lax.rem(me + n // 2, n)
    last = 2 * REACH
    mate_slot = last - last * side
    relay_slot = last * side

    def at(band):
        return pl.ds(pl.multiple_of(band * block, block), block)

    def padded(band):
        return at(band + 1)

    def remote(source, target, stream, band, device):
        return pltpu.make_async_remote_copy(
            src_ref=source,
            dst_ref=target,
            send_sem=send.at[stream, band],
            recv_sem=recv.at[stream, band],
            device_id={"patch": device},
            device_id_type=pl.DeviceIdType.MESH,
        )

    def keys_mate(band):
        own = kv.at[REACH, :, padded(band), :]
        return remote(own, kv.at[relay_slot, :, padded(band), :], 0, band, mate)

    def keys_relay(band):
        device = lax.rem(me + n + 4 - 8 * side, n)
        fetched = kv.at[mate_slot, :, padded(band), :]
        return remote(fetched, kv.at[relay_slot, :, padded(band), :], 1, band, device)

    def keys_near(band):
        own = kv.at[REACH, :, padded(band), :]
        return remote(own, kv.at[1 + 2 * odd, :, padded(band), :], 2, band, partner)

    def keys_far(band):
        fetched = kv.at[last - last * odd, :, padded(band), :]
        return remote(fetched, kv.at[3 - 2 * odd, :, padded(band), :], 3, band, partner)

    def sums_far(band):
        source = totals.at[1 + 2 * odd, :, padded(band), :]
        return remote(source, far_in.at[:, at(band), :], 4, band, partner)

    def sums_near(band):
        source = totals.at[3 - 2 * odd, :, padded(band), :]
        return remote(source, near_in.at[:, at(band), :], 5, band, partner)

    def sums_relay(band):
        device = lax.rem(me + n - 4 + 8 * side, n)
        return remote(relay_out.at[:, at(band), :], relay_in.at[:, at(band), :], 6, band, device)

    def sums_mate(band):
        return remote(mate_out.at[:, at(band), :], mate_in.at[:, at(band), :], 7, band, mate)

    def pole_copy(source, target, which):
        return pltpu.make_async_remote_copy(
            src_ref=source,
            dst_ref=target,
            send_sem=pole_send.at[which],
            recv_sem=pole_recv.at[which],
            device_id={"patch": across},
            device_id_type=pl.DeviceIdType.MESH,
        )

    def pole_keys(which):
        edge = 0 if which == 0 else bands - 1
        beyond = -1 if which == 0 else bands
        return pole_copy(kv.at[REACH, :, padded(edge), :], kv.at[REACH, :, padded(beyond), :], which)

    def pole_sums(which):
        return pole_copy(pole_out.at[which], pole_in.at[which], 2 + which)

    def each_band(body):
        def step(band, carry):
            body(band)
            return carry

        lax.fori_loop(0, bands, step, 0)

    def scaled(part, value):
        return value * jnp.float32(scale) if part == 0 else value

    barrier = pltpu.get_barrier_semaphore()
    for device in (mate, partner, ahead, behind, across):
        pl.semaphore_signal(
            barrier, inc=1, device_id={"patch": device}, device_id_type=pl.DeviceIdType.MESH
        )
    kv[REACH, 0, block : block + tokens, :] = key_rows[...]
    kv[REACH, 1, block : block + tokens, :] = value_rows[...]
    pl.semaphore_wait(barrier, 5)

    pole_keys(0).start()

    def send_keys(band):
        keys_mate(band).start()
        keys_near(band).start()

    for band in range(7):
        send_keys(band)

    blank = jnp.zeros((2, block, features), kv.dtype)
    for slot in range(SLOTS):
        if slot != REACH:
            kv[slot, :, :block, :] = blank
            kv[slot, :, block + tokens :, :] = blank
    for slot in range(SLOTS):
        for part in range(2):
            totals[slot, part] = jnp.zeros(totals.shape[2:], jnp.float32)

    def send_pole_sums(which, beyond):
        for part in range(2):
            value = scaled(part, totals[REACH, part, padded(beyond), :])
            pole_out[which, part] = value.astype(jnp.bfloat16)
        pole_sums(which).start()

    def step(t, carry):
        @pl.when(t < bands - 7)
        def _():
            send_keys(t + 7)

        @pl.when(t == bands - 7)
        def _():
            pole_keys(1).start()

        @pl.when(t < bands)
        def _():
            keys_mate(t).wait_recv()
            keys_relay(t).start()

        @pl.when((t >= 3) & (t < bands + 3))
        def _():
            keys_near(t - 3).wait_recv()
            keys_relay(t - 3).wait_recv()
            keys_far(t - 3).start()

        @pl.when((t >= 4) & (t < bands + 4))
        def _():
            keys_far(t - 4).wait_recv()

        @pl.when(t == 5)
        def _():
            pole_keys(0).wait_recv()

        @pl.when(t == bands + 4)
        def _():
            pole_keys(1).wait_recv()

        @pl.when((t >= 5) & (t < bands + 5))
        def _():
            attend_band(
                t - 5, block, bias, queries, grad_out, kv, totals, grad_queries, probs, grads
            )

        @pl.when(t == 6)
        def _():
            send_pole_sums(0, -1)

        @pl.when(t == bands + 5)
        def _():
            send_pole_sums(1, bands)

        @pl.when((t >= 6) & (t < bands + 6))
        def _():
            sums_far(t - 6).start()
            sums_near(t - 6).start()

        @pl.when((t >= 8) & (t < bands + 8))
        def _():
            band = t - 8
            sums_far(band).wait_recv()
            for part in range(2):
                totals[last - last * odd, part, padded(band), :] += far_in[part, at(band), :]
                value = scaled(part, totals[relay_slot, part, padded(band), :])
                relay_out[part, at(band), :] = value.astype(jnp.bfloat16)
            sums_relay(band).start()

        @pl.when(t >= 11)
        def _():
            band = t - 11
            sums_relay(band).wait_recv()
            for part in range(2):
                value = scaled(part, totals[mate_slot, part, padded(band), :])
                value = value + relay_in[part, at(band), :].astype(jnp.float32)
                mate_out[part, at(band), :] = value.astype(jnp.bfloat16)
            sums_mate(band).start()

        return carry

    lax.fori_loop(0, bands + 11, step, 0)

    @each_band
    def _(band):
        sums_near(band).wait_recv()
        sums_mate(band).wait_recv()
        for part, result in ((0, grad_keys), (1, grad_values)):
            value = totals[REACH, part, padded(band), :] + near_in[part, at(band), :]
            arrived = mate_in[part, at(band), :].astype(jnp.float32)
            result[at(band), :] = scaled(part, value) + arrived

    for which, edge in ((0, 0), (1, bands - 1)):
        pole_sums(which).wait_recv()
        for part, result in ((0, grad_keys), (1, grad_values)):
            result[at(edge), :] += pole_in[which, part].astype(jnp.float32)

    @each_band
    def _(band):
        for copy in (keys_mate, keys_relay, keys_near, keys_far):
            copy(band).wait_send()
        for copy in (sums_far, sums_near, sums_relay, sums_mate):
            copy(band).wait_send()

    for which in range(2):
        pole_keys(which).wait_send()
        pole_sums(which).wait_send()


def bias_of(window_blocks):
    bands = window_blocks.shape[0]
    stripes = lax.axis_size("patch")
    stripe = lax.axis_index("patch")
    band = jnp.arange(bands, dtype=jnp.int32)[:, None, None]
    slot = jnp.arange(SLOTS, dtype=jnp.int32)[None, :, None]
    row = band + jnp.arange(-1, 2, dtype=jnp.int32)[None, None, :]
    inside = (row >= 0) & (row < bands)
    regular = (stripe + slot - REACH) % stripes * bands + row
    across = jnp.where(slot == REACH, (stripe + stripes // 2) % stripes * bands + band, -2)
    wanted = jnp.where(inside, regular, across)
    live = jnp.any(wanted[..., None] == window_blocks[:, None, None, :], axis=-1)
    return jnp.where(live, 0.0, -1e30).astype(jnp.float32).reshape(bands, SLOTS * 3)


def local(queries, key_rows, value_rows, grad_out, window_blocks):
    tokens, features = queries.shape
    bands = window_blocks.shape[0]
    block = tokens // bands
    vmem = pl.BlockSpec(memory_space=pltpu.VMEM)
    result = jax.ShapeDtypeStruct((tokens, features), jnp.float32)
    padded = tokens + 2 * block
    wide = pltpu.VMEM((SLOTS * 3 * block, HEADS * block), jnp.float32)
    whole = pltpu.VMEM((2, tokens, features), jnp.float32)
    travelling = pltpu.VMEM((2, tokens, features), jnp.bfloat16)
    pole = pltpu.VMEM((2, 2, block, features), jnp.bfloat16)
    return pl.pallas_call(
        functools.partial(kernel, block),
        out_shape=(result, result, result),
        in_specs=[pl.BlockSpec(memory_space=pltpu.SMEM), vmem, vmem, vmem, vmem],
        out_specs=(vmem, vmem, vmem),
        scratch_shapes=[
            pltpu.VMEM((SLOTS, 2, padded, features), jnp.bfloat16),
            pltpu.VMEM((SLOTS, 2, padded, features), jnp.float32),
            wide,
            wide,
            whole,
            whole,
            *([travelling] * 4),
            pole,
            pole,
            pltpu.SemaphoreType.DMA((8, bands)),
            pltpu.SemaphoreType.DMA((8, bands)),
            pltpu.SemaphoreType.DMA((4,)),
            pltpu.SemaphoreType.DMA((4,)),
        ],
        compiler_params=pltpu.CompilerParams(
            collective_id=0, has_side_effects=True, vmem_limit_bytes=60 * 2**20
        ),
    )(bias_of(window_blocks), queries, grad_out, key_rows, value_rows)


def solution(mesh):
    spec = P(("group", "patch"), None)
    return jax.shard_map(
        local,
        mesh=mesh,
        in_specs=(spec, spec, spec, spec, P("patch", None)),
        out_specs=(spec, spec, spec),
        check_vma=False,
    )
```
